32 devices in a mesh: dp: 2 (over core), pipe: 2 (over x), expert: 8 (over z, y).
Axes of the slice: x: 2, y: 2, z: 4, core: 2. Of those that a mesh axis runs over, the one named last changes fastest.
Arguments:
- saved_inputs: bfloat16 [2, 4, 128, 3072], P('pipe', None, 'dp'), may hold values from -6 to 6
- top_grad: bfloat16 [4, 128, 3072], P(None, 'dp'), may hold values from -6 to 6
- routes: int32 [2, 4, 128, 2], P('pipe', None, 'dp'), may hold values from 0 to 3, all different within a row; in each aligned block of 64 rows (0 to 63, 64 to 127, ..., all dimensions but the last counted through in order) at most 48 rows name the same one
- mix_weights: float32 [2, 4, 128, 2], P('pipe', None, 'dp'), may hold values from 0.2 to 0.8
- w_gate: bfloat16 [2, 8, 1, 3072, 4096], P('pipe', 'expert', None, None, 'dp'), may hold values from -0.109375 to 0.109375
- w_up: bfloat16 [2, 8, 1, 3072, 4096], P('pipe', 'expert', None, None, 'dp'), may hold values from -0.109375 to 0.109375
- w_down: bfloat16 [2, 8, 1, 4096, 3072], P('pipe', 'expert', None, 'dp'), may hold values from -0.0625 to 0.0625
- q_prev: float32 [2, 8, 1, 3, 4096, 64], P('pipe', 'expert', None, None, 'dp'), may hold values from -6 to 6
Outputs:
- input_grads: bfloat16 [2, 4, 128, 3072], P('pipe', None, 'dp')
- basis: float32 [2, 8, 1, 3072, 64], P('pipe', 'expert', None, 'dp')
- q_next: float32 [2, 8, 1, 3, 4096, 64], P('pipe', 'expert', None, None, 'dp')
The draws below stay inside these ranges and needn't reach their ends.
Inputs may be any that keep to these rules, and one draw needn't show every extreme that they name: For every section, microbatch and aligned block of 64 tokens (the tokens of one index of dp), each expert is named by at most 48 routes, a bound that some block reaches; a token's 2 routes name different experts.
All inputs are finite; a program needn't handle non-finite values.
Results may differ from the reference program's by a relative error of at most 0.015.
Values may be sent and summed in bfloat16 or wider, within the bound.
A program may use at most 192 MiB of HBM per device.

```python
import math
import jax
import jax.numpy as jnp
import numpy as np
from jax import lax

D = 3072
EXPERTS = 4
F = 8192
TOP = 2
R = 64
MICRO = 4
TOK_DEV = 64
EXP_DEV = 1
COPY = 2
FSLICE = 4096
CAP = 48
TOKENS = 128
SECTIONS = 2
N_DP = 2
N_PIPE = 2
N_EXPERT = 8


def block_levels(stream_key, extent, cuts, smallest, largest):
    factor_of, own = 1.0, jax.random.fold_in(stream_key, 6)
    for position, blocks in cuts:
        heights = jnp.exp(jax.random.uniform(jax.random.fold_in(own, position), (blocks,), jnp.float32, smallest / len(cuts), largest / len(cuts)))
        factor_of = factor_of * jnp.repeat(heights, extent[position] // blocks).reshape([-1 if axis == position else 1 for axis in range(len(extent))])
    return factor_of


def shared_out(own_key, own, number, rows, number_of, top, reach, lean):
    sequence = jax.random.permutation(own_key, number_of)
    heavy_load, ordinary = load_shares(number_of, rows * top, reach, lean, True), load_shares(number_of, rows * top, reach, lean, False)
    places = jnp.arange(number_of)

    def named(sizes, turn):
        used = int((sizes > 0).sum())
        fixed = max(1, used // 4)
        passed = fixed + (places - fixed + turn * (used - fixed)) % max(1, number_of - fixed)
        return jnp.zeros((number_of,), jnp.int32).at[sequence[jnp.where(places < fixed, places, passed)]].set(jnp.asarray(sizes, jnp.int32))

    sizes = jnp.where(number % 4 == 0, named(heavy_load, number // 4), named(ordinary, number - number // 4 - 1))
    mixed = jax.random.permutation(jax.random.fold_in(own, 3), number_of)
    donor, sink = mixed[0:number_of // 2 * 2:2], mixed[1:number_of // 2 * 2:2]
    slack = jnp.minimum(sizes[donor] - 1, reach - sizes[sink]) // 2
    slack = jnp.where((donor == sequence[0]) | (sink == sequence[0]) | (sizes[sink] == 0), 0, jnp.maximum(slack, 0))
    passed = jax.random.randint(jax.random.fold_in(own, 4), (number_of // 2,), 0, 1 << 20) % (slack + 1)
    sizes = sizes.at[donor].add(-passed).at[sink].add(passed)
    items = jnp.searchsorted(jnp.cumsum(sizes), jnp.arange(rows * top), side="right").astype(jnp.int32)
    listing = items.reshape(top, rows).T
    listing = listing[jax.random.permutation(jax.random.fold_in(own, 1), rows)]
    turn = jax.random.randint(jax.random.fold_in(own, 2), (rows, 1), 0, top)
    return jnp.take_along_axis(listing, (jnp.arange(top)[None, :] + turn) % top, axis=1)


def load_shares(number_of, total, reach, lean, full):
    loads = [(1 << 20) // math.isqrt(rank ** lean) + 1 for rank in range(1, number_of + 1)]
    largest = reach if full else min(reach, max(-(-total // number_of), total * loads[0] // sum(loads)))
    least = 1 if total - largest >= number_of - 1 else 0
    holding, surplus = [largest] + [least] * (number_of - 1), total - largest - least * (number_of - 1)
    while surplus > 0:
        movable = [i for i in range(1, number_of) if holding[i] < largest] or [i for i in range(1, number_of) if holding[i] < reach]
        whole, remaining = sum([loads[i] for i in movable]), surplus
        for i in movable:
            addition = min(reach - holding[i], max(1, remaining * loads[i] // whole), surplus)
            holding[i] = holding[i] + addition
            surplus = surplus - addition
    return np.array(holding)


def centred(rng, shape, spread, reach, pieces=(), held_as=jnp.bfloat16):
    values = jax.random.normal(rng, shape, jnp.float32) * spread
    if len(pieces) > 0:
        values = block_levels(rng, shape, pieces, -0.22, 0.18) * values
    return jnp.clip(values, min=-reach, max=reach).astype(held_as)


def setup_inputs(seed: int = 0) -> dict:
    keys = jax.random.split(jax.random.key(seed), 9)
    saved_inputs = centred(keys[0], (SECTIONS, MICRO, TOKENS, D), 1.0, 6.0, ((0, 2), (2, 2)))
    top_grad = centred(keys[1], (MICRO, TOKENS, D), 1.0, 6.0, ((1, 2),))
    routes_keys = jax.random.split(jax.random.fold_in(keys[2], 1), SECTIONS * MICRO * TOKENS // TOK_DEV)
    routes_turns = jax.random.permutation(jax.random.fold_in(keys[2], 3), SECTIONS * MICRO * TOKENS // TOK_DEV)
    routes = jax.vmap(lambda own, number: shared_out(jax.random.fold_in(keys[2], 2), own, number, TOK_DEV, EXPERTS, TOP, CAP, 2))(routes_keys, routes_turns).reshape((SECTIONS, MICRO, TOKENS, TOP))
    mix_weights = jnp.clip(0.2 + 0.6 * jax.random.uniform(keys[3], (SECTIONS, MICRO, TOKENS, TOP), jnp.float32) ** block_levels(keys[3], (SECTIONS, MICRO, TOKENS, TOP), ((0, 2), (2, 2)), -0.2, 0.2), 0.2, 0.8)
    w_gate = centred(keys[4], (SECTIONS, N_EXPERT, EXP_DEV, D, FSLICE), D ** -0.5, 0.109375, ((0, 2), (1, 8), (4, 2)))
    w_up = centred(keys[5], (SECTIONS, N_EXPERT, EXP_DEV, D, FSLICE), D ** -0.5, 0.109375, ((0, 2), (1, 8), (4, 2)))
    w_down = centred(keys[6], (SECTIONS, N_EXPERT, EXP_DEV, FSLICE, D), F ** -0.5, 0.0625, ((0, 2), (1, 8), (3, 2)))
    q_prev = centred(keys[7], (SECTIONS, N_EXPERT, EXP_DEV, 3, FSLICE, R), 1.0, 6.0, ((0, 2), (1, 8), (4, 2)), jnp.float32)
    return dict(saved_inputs=saved_inputs, top_grad=top_grad, routes=routes, mix_weights=mix_weights, w_gate=w_gate, w_up=w_up, w_down=w_down, q_prev=q_prev)


def slot_tables(route_rows, mix_rows):
    token_count = route_rows.shape[0]
    flat_routes = route_rows.reshape(-1).astype(jnp.int32)
    one_hot = (flat_routes[:, None] == jnp.arange(EXPERTS, dtype=jnp.int32)[None, :]).astype(jnp.int32)
    rank_in_expert = lax.optimization_barrier(jnp.sum(jnp.cumsum(one_hot, axis=0) * one_hot, axis=1)) - 1
    slot_ids = flat_routes * CAP + rank_in_expert
    slot_hits = (slot_ids[:, None] == jnp.arange(EXPERTS * CAP, dtype=jnp.int32)[None, :]).astype(jnp.float32)
    slot_hits = slot_hits.reshape(token_count, TOP, EXPERTS * CAP)
    picker = lax.optimization_barrier(jnp.sum(slot_hits, axis=1)).T
    weigher = lax.optimization_barrier(jnp.sum(slot_hits * mix_rows[:, :, None].astype(jnp.float32), axis=1)).T
    return (picker, weigher)

def expert_grads(input_rows, grad_rows, gate_weight, up_weight, down_weight):
    pre_gate = jnp.dot(input_rows.astype(jnp.float32), gate_weight.astype(jnp.float32), preferred_element_type=jnp.float32)
    pre_up = jnp.dot(input_rows.astype(jnp.float32), up_weight.astype(jnp.float32), preferred_element_type=jnp.float32)
    sigmoid_gate = jax.nn.sigmoid(pre_gate)
    silu_gate = pre_gate * sigmoid_gate
    hidden = (silu_gate * pre_up).astype(jnp.bfloat16)
    grad_hidden = lax.dot_general(grad_rows.astype(jnp.float32), down_weight.astype(jnp.float32), (((1,), (1,)), ((), ())), preferred_element_type=jnp.float32)
    grad_gate = (grad_hidden * pre_up * sigmoid_gate * (1.0 + pre_gate * (1.0 - sigmoid_gate))).astype(jnp.bfloat16)
    grad_up = (grad_hidden * silu_gate).astype(jnp.bfloat16)
    input_rows_grad = lax.dot_general(grad_gate.astype(jnp.float32), gate_weight.astype(jnp.float32), (((1,), (1,)), ((), ())), preferred_element_type=jnp.float32)
    input_rows_grad = input_rows_grad + lax.dot_general(grad_up.astype(jnp.float32), up_weight.astype(jnp.float32), (((1,), (1,)), ((), ())), preferred_element_type=jnp.float32)
    gate_total = lax.dot_general(input_rows.astype(jnp.float32), grad_gate.astype(jnp.float32), (((0,), (0,)), ((), ())), preferred_element_type=jnp.float32)
    up_total = lax.dot_general(input_rows.astype(jnp.float32), grad_up.astype(jnp.float32), (((0,), (0,)), ((), ())), preferred_element_type=jnp.float32)
    down_total = lax.dot_general(grad_rows.astype(jnp.float32), hidden.astype(jnp.float32), (((0,), (0,)), ((), ())), preferred_element_type=jnp.float32)
    return (input_rows_grad, gate_total, up_total, down_total)

def orthonormal(lower_factor, factor):
    return jax.scipy.linalg.solve_triangular(lower_factor, factor.T, lower=True).T

def reference(saved_inputs, top_grad, routes, mix_weights, w_gate, w_up, w_down, q_prev):
    blocks = N_DP
    groups = N_EXPERT // COPY
    highest = lax.Precision.HIGHEST
    arriving_all = top_grad
    grads_list, basis_list, q_list = ([], [], [])
    for section_index in range(N_PIPE - 1, -1, -1):
        gate_section = w_gate[section_index].reshape(groups, COPY, EXP_DEV, D, FSLICE).transpose(0, 2, 3, 1, 4).reshape(EXPERTS, D, F)
        up_section = w_up[section_index].reshape(groups, COPY, EXP_DEV, D, FSLICE).transpose(0, 2, 3, 1, 4).reshape(EXPERTS, D, F)
        down_section = w_down[section_index].reshape(groups, COPY, EXP_DEV, FSLICE, D).transpose(0, 2, 1, 3, 4).reshape(EXPERTS, F, D)
        right_section = q_prev[section_index].reshape(groups, COPY, EXP_DEV, 3, FSLICE, R).transpose(0, 2, 3, 1, 4, 5).reshape(EXPERTS, 3, F, R)

        def regroup(slots):
            slots = slots.reshape(blocks, EXPERTS, CAP, D).transpose(1, 0, 2, 3)
            return slots.reshape(EXPERTS, blocks * CAP, D)

        def per_expert(inputs):
            return expert_grads(inputs[0], inputs[1], inputs[2], inputs[3], inputs[4])

        def one_micro(totals, inputs):
            tokens_in, arriving, route_micro, mix_micro = inputs
            input_blocks = tokens_in.reshape(blocks, TOK_DEV, D).astype(jnp.float32)
            arriving_blocks = arriving.reshape(blocks, TOK_DEV, D).astype(jnp.float32)
            pickers, weighers = jax.vmap(slot_tables)(route_micro.reshape(blocks, TOK_DEV, TOP), mix_micro.reshape(blocks, TOK_DEV, TOP))
            input_slots = jnp.einsum('bjt,btd->bjd', pickers, input_blocks, precision=highest).astype(jnp.bfloat16)
            grad_slots = jnp.einsum('bjt,btd->bjd', weighers, arriving_blocks, precision=highest).astype(jnp.bfloat16)
            slot_grads, gate_total, up_total, down_total = lax.map(per_expert, (regroup(input_slots), regroup(grad_slots), gate_section, up_section, down_section))
            slot_grads = slot_grads.reshape(EXPERTS, blocks, CAP, D).transpose(1, 0, 2, 3).reshape(blocks, EXPERTS * CAP, D)
            combined = arriving_blocks + jnp.einsum('bjt,bjd->btd', pickers, slot_grads, precision=highest)
            totals = (totals[0] + gate_total, totals[1] + up_total, totals[2] + down_total)
            return (totals, combined.astype(jnp.bfloat16).reshape(TOKENS, D))
        empty_grad = jnp.zeros((EXPERTS, D, F), jnp.float32)
        totals, section_grads = lax.scan(one_micro, (empty_grad, empty_grad, empty_grad), (saved_inputs[section_index], arriving_all, routes[section_index], mix_weights[section_index]))
        arriving_all = section_grads
        factor = jnp.einsum('edf,efr->edr', totals[0], right_section[:, 0], precision=highest)
        factor = factor + jnp.einsum('edf,efr->edr', totals[1], right_section[:, 1], precision=highest)
        factor = factor + jnp.einsum('edf,efr->edr', totals[2], right_section[:, 2], precision=highest)
        gram_matrix = jnp.einsum('edr,eds->ers', factor, factor, precision=highest)
        lower_factor = jnp.linalg.cholesky(gram_matrix)
        ortho = jax.vmap(orthonormal)(lower_factor, factor)
        scale_back = math.sqrt(float(MICRO * TOKENS))
        q_parts = [jnp.einsum('edf,edr->efr', totals[part], ortho, precision=highest) / scale_back for part in range(3)]
        q_new = jnp.stack(q_parts, axis=1)
        q_new = q_new.reshape(groups, EXP_DEV, 3, COPY, FSLICE, R).transpose(0, 3, 1, 2, 4, 5).reshape(N_EXPERT, EXP_DEV, 3, FSLICE, R)
        basis_now = (ortho * math.sqrt(float(D))).reshape(groups, 1, EXP_DEV, D, R)
        basis_now = jnp.broadcast_to(basis_now, (groups, COPY, EXP_DEV, D, R)).reshape(N_EXPERT, EXP_DEV, D, R)
        grads_list.insert(0, section_grads)
        basis_list.insert(0, basis_now)
        q_list.insert(0, q_new)
    return (jnp.stack(grads_list), jnp.stack(basis_list), jnp.stack(q_list))
```

```python
import math

import jax
import jax.numpy as jnp
from jax import lax
from jax.sharding import PartitionSpec as P

EXPERTS = 4
CHUNKS = 2


def swapped(block, axis, level):
    count = lax.axis_size(axis)
    return lax.ppermute(block, axis, [(i, i ^ (1 << level)) for i in range(count)])


def dot(a, b, contract):
    return lax.dot_general(a, b, (contract, ((), ())), preferred_element_type=jnp.float32)


def split(value, axis):
    high = value.astype(jnp.bfloat16)
    low = (value - high.astype(jnp.float32)).astype(jnp.bfloat16)
    return jnp.concatenate([high, low], axis=axis)


def joined(value, axis):
    half = value.shape[axis] // 2
    return lax.slice_in_dim(value, 0, half, axis=axis) + lax.slice_in_dim(
        value, half, 2 * half, axis=axis
    )


def half_of(rows, which):
    count = rows.shape[0] // 2
    return lax.dynamic_slice_in_dim(rows, which * count, count, 0)


def scattered(own_half, partner_half, arriving):
    total = own_half + swapped(partner_half.astype(jnp.bfloat16), "dp", 0).astype(jnp.float32)
    index = lax.axis_index("expert")
    for level in range(lax.axis_size("expert").bit_length() - 1):
        bit = (index >> level) & 1
        total = total.astype(jnp.bfloat16)
        other = swapped(half_of(total, 1 - bit), "expert", level)
        total = half_of(total, bit).astype(jnp.float32) + other.astype(jnp.float32)
        arriving = half_of(arriving, bit)
    return (arriving.astype(jnp.float32) + total).astype(jnp.bfloat16)


def gathered(rows):
    index = lax.axis_index("expert")
    for level in reversed(range(lax.axis_size("expert").bit_length() - 1)):
        bit = (index >> level) & 1
        other = swapped(rows, "expert", level)
        first = jnp.where(bit == 0, rows, other)
        second = jnp.where(bit == 0, other, rows)
        rows = jnp.concatenate([first, second], axis=0)
    return rows


def shards(saved_inputs, top_grad, routes, mix_weights, w_gate, w_up, w_down, q_prev):
    highest = lax.Precision.HIGHEST
    sections = lax.axis_size("pipe")
    section_index = lax.axis_index("pipe")
    expert_groups = lax.axis_size("expert")
    replicas = lax.axis_size("dp")
    gate, up, down, right = w_gate[0, 0, 0], w_up[0, 0, 0], w_down[0, 0, 0], q_prev[0, 0, 0]
    copies = expert_groups // EXPERTS
    expert = lax.axis_index("expert") // copies
    micro, token_count, width = top_grad.shape
    chunk_rows = micro // CHUNKS * token_count

    inputs_own = saved_inputs[0].reshape(CHUNKS, chunk_rows, width)
    weight_own = jnp.sum(jnp.where(routes[0] == expert, mix_weights[0], 0.0), axis=-1)
    weight_own = weight_own.reshape(CHUNKS, chunk_rows)
    inputs_all = jnp.stack([inputs_own, swapped(inputs_own, "dp", 0)], axis=1)
    weight_all = jnp.stack([weight_own, swapped(weight_own, "dp", 0)], axis=1)
    input_rows = inputs_all.reshape(CHUNKS * 2 * chunk_rows, width)

    pre_gate = dot(input_rows, gate, ((1,), (0,)))
    pre_up = dot(input_rows, up, ((1,), (0,)))
    sigmoid_gate = jax.nn.sigmoid(pre_gate)
    silu_gate = pre_gate * sigmoid_gate
    hidden = (silu_gate * pre_up).astype(jnp.bfloat16)
    slope = pre_up * sigmoid_gate * (1.0 + pre_gate * (1.0 - sigmoid_gate))

    arriving = [top_grad.reshape(CHUNKS, chunk_rows, width)[c] for c in range(CHUNKS)]
    produced = [None] * CHUNKS
    kept = [None] * CHUNKS
    for stage in range(sections):
        active = section_index == sections - 1 - stage
        upcoming = []
        for c in range(CHUNKS):
            block = slice(c * 2 * chunk_rows, (c + 1) * 2 * chunk_rows)
            both = jnp.stack([arriving[c], swapped(arriving[c], "dp", 0)])
            grad_rows = (weight_all[c][:, :, None] * both.astype(jnp.float32)).astype(jnp.bfloat16)
            grad_rows = grad_rows.reshape(2 * chunk_rows, width)
            grad_hidden = dot(grad_rows, down, ((1,), (1,)))
            grad_gate = (grad_hidden * slope[block]).astype(jnp.bfloat16)
            grad_up = (grad_hidden * silu_gate[block]).astype(jnp.bfloat16)
            rows_grad = dot(grad_gate, gate, ((1,), (1,))) + dot(grad_up, up, ((1,), (1,)))
            share = scattered(rows_grad[:chunk_rows], rows_grad[chunk_rows:], arriving[c])
            fresh = (grad_rows, grad_gate, grad_up)
            if stage == 0:
                kept[c] = fresh
            else:
                kept[c] = tuple(jnp.where(active, a, b) for a, b in zip(fresh, kept[c]))
            if stage + 1 < sections:
                passed = lax.ppermute(share, "pipe", [(s, s - 1) for s in range(1, sections)])
                share = jnp.where(active, share, passed)
            result = gathered(share)
            produced[c] = result if stage == 0 else jnp.where(active, result, produced[c])
            upcoming.append(result)
        arriving = upcoming

    grad_rows, grad_gate, grad_up = (jnp.concatenate(parts, axis=0) for parts in zip(*kept))
    row_total = grad_rows.shape[0]
    outer_rows = jnp.concatenate([input_rows, grad_rows], axis=0)
    left = joined(
        dot(grad_gate, split(right[0], 1), ((1,), (0,)))
        + dot(grad_up, split(right[1], 1), ((1,), (0,))),
        1,
    )
    last = joined(dot(hidden, split(right[2], 1), ((1,), (0,))), 1)
    inner = jnp.stack([left, last]).reshape(2 * CHUNKS, 2, chunk_rows, -1)
    inner = inner + swapped(inner, "dp", 0)[:, ::-1]
    for level in range(copies.bit_length() - 1):
        inner = inner.astype(jnp.bfloat16)
        inner = inner.astype(jnp.float32) + swapped(inner, "expert", level).astype(jnp.float32)
    inner = inner.reshape(2 * row_total, -1)
    factor = joined(dot(split(inner, 1), outer_rows, ((0,), (0,))), 0)
    gram = lax.dot_general(factor, factor, (((1,), (1,)), ((), ())), precision=highest)
    lower = jnp.linalg.cholesky(gram)
    ortho = jax.scipy.linalg.solve_triangular(lower, factor, lower=True)
    mixed = joined(dot(outer_rows, split(ortho, 0), ((1,), (1,))), 1)
    mixed = mixed / math.sqrt(float(micro * token_count * replicas))
    first, second = split(mixed[:row_total], 1), split(mixed[row_total:], 1)
    q_next = jnp.stack(
        [
            joined(dot(grad_gate, first, ((0,), (0,))), 1),
            joined(dot(grad_up, first, ((0,), (0,))), 1),
            joined(dot(hidden, second, ((0,), (0,))), 1),
        ]
    )
    basis_rows = width // replicas
    basis = lax.dynamic_slice_in_dim(ortho, lax.axis_index("dp") * basis_rows, basis_rows, 1)
    basis = basis.T * math.sqrt(float(width))
    grads = jnp.stack(produced).reshape(micro, token_count, width)
    return (grads[None], basis[None, None, None], q_next[None, None, None])


def solution(mesh):
    placed = (
        P("pipe", None, "dp", None),
        P(None, "dp", None),
        P("pipe", None, "dp", None),
        P("pipe", None, "dp", None),
        P("pipe", "expert", None, None, "dp"),
        P("pipe", "expert", None, None, "dp"),
        P("pipe", "expert", None, "dp", None),
        P("pipe", "expert", None, None, "dp", None),
    )
    return jax.shard_map(
        shards,
        mesh=mesh,
        in_specs=placed,
        out_specs=(
            P("pipe", None, "dp", None),
            P("pipe", "expert", None, "dp", None),
            P("pipe", "expert", None, None, "dp", None),
        ),
        check_vma=False,
    )
```

```python
import math

import jax
import jax.numpy as jnp
from jax import lax
from jax.sharding import PartitionSpec as P

EXPERTS = 4
CHUNKS = 2


def swapped(block, axis, level):
    count = lax.axis_size(axis)
    return lax.ppermute(block, axis, [(i, i ^ (1 << level)) for i in range(count)])


def dot(a, b, contract):
    return lax.dot_general(a, b, (contract, ((), ())), preferred_element_type=jnp.float32)


def split(value, axis):
    high = value.astype(jnp.bfloat16)
    low = (value - high.astype(jnp.float32)).astype(jnp.bfloat16)
    return jnp.concatenate([high, low], axis=axis)


def joined(value, axis):
    half = value.shape[axis] // 2
    return lax.slice_in_dim(value, 0, half, axis=axis) + lax.slice_in_dim(
        value, half, 2 * half, axis=axis
    )


def half_of(rows, which):
    count = rows.shape[0] // 2
    return lax.dynamic_slice_in_dim(rows, which * count, count, 0)


def tie(first, second):
    return lax.optimization_barrier((first, second))


def exchanged(block, axis, level, queue):
    other = swapped(block, axis, level)
    return beside(block, other, queue)


def beside(block, other, queue):
    if queue:
        other = queue.pop(0)(block, other)
    return other


def scattered(own_half, partner_half, arriving, queue):
    total = own_half + swapped(partner_half.astype(jnp.bfloat16), "dp", 0).astype(jnp.float32)
    index = lax.axis_index("expert")
    for level in range(lax.axis_size("expert").bit_length() - 1):
        bit = (index >> level) & 1
        total = total.astype(jnp.bfloat16)
        other = exchanged(half_of(total, 1 - bit), "expert", level, queue)
        total = half_of(total, bit).astype(jnp.float32) + other.astype(jnp.float32)
        arriving = half_of(arriving, bit)
    return (arriving.astype(jnp.float32) + total).astype(jnp.bfloat16)


def gathered(rows, queue):
    index = lax.axis_index("expert")
    for level in reversed(range(lax.axis_size("expert").bit_length() - 1)):
        bit = (index >> level) & 1
        other = exchanged(rows, "expert", level, queue)
        first = jnp.where(bit == 0, rows, other)
        second = jnp.where(bit == 0, other, rows)
        rows = jnp.concatenate([first, second], axis=0)
    return rows


def shards(saved_inputs, top_grad, routes, mix_weights, w_gate, w_up, w_down, q_prev):
    highest = lax.Precision.HIGHEST
    sections = lax.axis_size("pipe")
    section_index = lax.axis_index("pipe")
    expert_groups = lax.axis_size("expert")
    replicas = lax.axis_size("dp")
    gate, up, down, right = w_gate[0, 0, 0], w_up[0, 0, 0], w_down[0, 0, 0], q_prev[0, 0, 0]
    copies = expert_groups // EXPERTS
    expert = lax.axis_index("expert") // copies
    micro, token_count, width = top_grad.shape
    chunk_rows = micro // CHUNKS * token_count

    inputs_own = saved_inputs[0].reshape(CHUNKS, chunk_rows, width)
    weight_own = jnp.sum(jnp.where(routes[0] == expert, mix_weights[0], 0.0), axis=-1)
    weight_own = weight_own.reshape(CHUNKS, chunk_rows)
    weight_all = jnp.stack([weight_own, swapped(weight_own, "dp", 0)], axis=1)
    input_rows = [
        jnp.concatenate([inputs_own[c], swapped(inputs_own[c], "dp", 0)], axis=0)
        for c in range(CHUNKS)
    ]
    arriving = [top_grad.reshape(CHUNKS, chunk_rows, width)[c] for c in range(CHUNKS)]
    kept = [None] * CHUNKS
    ahead = [{} for _ in range(CHUNKS)]
    tail = {}

    def piece(compute, operand, holder, name):
        def run(block=None, other=None):
            value = operand()
            if block is None:
                holder[name] = compute(value)
                return None
            value, _ = tie(value, block)
            holder[name], other = tie(compute(value), other)
            return other

        return run

    def forward_pieces(c):
        def gate_part(rows):
            return dot(rows, gate, ((1,), (0,)))

        def up_part(rows):
            pre_gate, pre_up = ahead[c]["gate"], dot(rows, up, ((1,), (0,)))
            sigmoid_gate = jax.nn.sigmoid(pre_gate)
            silu_gate = pre_gate * sigmoid_gate
            hidden = (silu_gate * pre_up).astype(jnp.bfloat16)
            slope = pre_up * sigmoid_gate * (1.0 + pre_gate * (1.0 - sigmoid_gate))
            return silu_gate, slope, hidden

        return [
            piece(gate_part, lambda: input_rows[c], ahead[c], "gate"),
            piece(up_part, lambda: input_rows[c], ahead[c], "forward"),
        ]

    def backward_pieces(c, stage, arrived, holder):
        def hidden_part(both):
            both = both.reshape(2, chunk_rows, width).astype(jnp.float32)
            grad_rows = (weight_all[c][:, :, None] * both).astype(jnp.bfloat16)
            grad_rows = grad_rows.reshape(2 * chunk_rows, width)
            silu_gate, slope, _ = ahead[c]["forward"]
            grad_hidden = dot(grad_rows, down, ((1,), (1,)))
            grad_gate = (grad_hidden * slope).astype(jnp.bfloat16)
            grad_up = (grad_hidden * silu_gate).astype(jnp.bfloat16)
            return grad_rows, grad_gate, grad_up

        return [
            piece(hidden_part, arrived, holder, "grads"),
            piece(
                lambda rows: dot(rows, gate, ((1,), (1,))),
                lambda: holder["grads"][1],
                holder,
                "gate",
            ),
            piece(
                lambda rows: dot(rows, up, ((1,), (1,))) + holder["gate"],
                lambda: holder["grads"][2],
                holder,
                "rows",
            ),
        ]

    def inner_part(grads):
        grad_gate, grad_up, hidden = grads
        left = dot(grad_gate, split(right[0], 1), ((1,), (0,)))
        left = joined(left + dot(grad_up, split(right[1], 1), ((1,), (0,))), 1)
        last = joined(dot(hidden, split(right[2], 1), ((1,), (0,))), 1)
        inner = jnp.stack([left, last]).reshape(2 * CHUNKS, 2, chunk_rows, -1)
        inner = inner + swapped(inner, "dp", 0)[:, ::-1]
        for level in range(copies.bit_length() - 1):
            inner = inner.astype(jnp.bfloat16)
            inner = inner.astype(jnp.float32) + swapped(inner, "expert", level).astype(jnp.float32)
        return inner.reshape(-1, inner.shape[-1])

    def factor_part(inner):
        factor = joined(dot(split(inner, 1), tail["outer"], ((0,), (0,))), 0)
        gram = lax.dot_general(factor, factor, (((1,), (1,)), ((), ())), precision=highest)
        return factor, gram

    def ortho_part(value):
        factor, lower = value
        return jax.scipy.linalg.solve_triangular(lower, factor, lower=True)

    def mixed_part(ortho):
        mixed = joined(dot(tail["outer"], split(ortho, 0), ((1,), (1,))), 1)
        return mixed / math.sqrt(float(micro * token_count * replicas))

    def update_part(mixed):
        grad_gate, grad_up, hidden = tail["all"]
        half = mixed.shape[0] // 2
        first, second = split(mixed[:half], 1), split(mixed[half:], 1)
        return jnp.stack(
            [
                joined(dot(grad_gate, first, ((0,), (0,))), 1),
                joined(dot(grad_up, first, ((0,), (0,))), 1),
                joined(dot(hidden, second, ((0,), (0,))), 1),
            ]
        )

    def all_grads():
        grad_rows, grad_gate, grad_up = (jnp.concatenate(parts, axis=0) for parts in zip(*kept))
        hidden = jnp.concatenate([ahead[c]["forward"][2] for c in range(CHUNKS)], axis=0)
        tail["all"] = (grad_gate, grad_up, hidden)
        tail["outer"] = jnp.concatenate([*input_rows, grad_rows], axis=0)
        return tail["all"]

    tail_pieces = [
        piece(inner_part, all_grads, tail, "inner"),
        piece(factor_part, lambda: tail["inner"], tail, "factor"),
        piece(jnp.linalg.cholesky, lambda: tail["factor"][1], tail, "lower"),
        piece(ortho_part, lambda: (tail["factor"][0], tail["lower"]), tail, "ortho"),
        piece(mixed_part, lambda: tail["ortho"], tail, "mixed"),
        piece(update_part, lambda: tail["mixed"], tail, "update"),
    ]

    def arrived_first(c):
        return lambda: jnp.concatenate([arriving[c], swapped(arriving[c], "dp", 0)], axis=0)

    holders = [[{} for _ in range(CHUNKS)] for _ in range(sections)]
    works = []
    for stage in range(sections):
        for c in range(CHUNKS):
            work = forward_pieces(c) if stage == 0 else []
            works.append(work + backward_pieces(c, stage, arrived_first(c), holders[stage][c]))
    works.append(tail_pieces)
    for run in works[0]:
        run()
    produced = [None] * CHUNKS
    for stage in range(sections):
        active = section_index == sections - 1 - stage
        for c in range(CHUNKS):
            queue = works[stage * CHUNKS + c + 1]
            holder = holders[stage][c]
            fresh = holder["grads"]
            if stage == 0:
                kept[c] = fresh
            else:
                kept[c] = tuple(jnp.where(active, a, b) for a, b in zip(fresh, kept[c]))
            rows_grad = holder["rows"]
            share = scattered(rows_grad[:chunk_rows], rows_grad[chunk_rows:], arriving[c], queue)
            if stage + 1 < sections:
                passed = lax.ppermute(share, "pipe", [(s, s - 1) for s in range(1, sections)])
                share = jnp.where(active, share, passed)
            result = gathered(share, queue)
            while queue:
                queue.pop(0)()
            produced[c] = result if stage == 0 else jnp.where(active, result, produced[c])
            arriving[c] = result

    basis_rows = width // replicas
    start = lax.axis_index("dp") * basis_rows
    basis = lax.dynamic_slice_in_dim(tail["ortho"], start, basis_rows, 1)
    basis = basis.T * math.sqrt(float(width))
    grads = jnp.stack(produced).reshape(micro, token_count, width)
    return (grads[None], basis[None, None, None], tail["update"][None, None, None])


def solution(mesh):
    placed = (
        P("pipe", None, "dp", None),
        P(None, "dp", None),
        P("pipe", None, "dp", None),
        P("pipe", None, "dp", None),
        P("pipe", "expert", None, None, "dp"),
        P("pipe", "expert", None, None, "dp"),
        P("pipe", "expert", None, "dp", None),
        P("pipe", "expert", None, None, "dp", None),
    )
    return jax.shard_map(
        shards,
        mesh=mesh,
        in_specs=placed,
        out_specs=(
            P("pipe", None, "dp", None),
            P("pipe", "expert", None, "dp", None),
            P("pipe", "expert", None, None, "dp", None),
        ),
        check_vma=False,
    )
```
